256 devices in a mesh: row: 32 (over x, y, core), col: 8 (over z).
Axes of the slice: x: 4, y: 4, z: 8, core: 2. Of those that a mesh axis runs over, the one named last changes fastest.
Arguments:
- panels: bfloat16 [1024, 512, 512], P('row', 'col'), may hold values from -6 to 6
- reader_row: int32 [1024, 1], P('row'), may hold values from 0 to 31; in each aligned block of 32 rows (0 to 31, 32 to 63, ...) at most 2 rows name the same one
- tile_offset: int32 [1024], P('row'), may hold values from 0 to 3
- schur_adjoint: bfloat16 [128, 512, 512], P('row'), may hold values from -0.1875 to 0.1875
- panel_adjoint: bfloat16 [1024, 512, 512], P('row', 'col'), may hold values from -6 to 6
- diag_inverse: bfloat16 [512, 512], P(None, 'col'), may hold values from -1 to 1.4, as said below
Outputs:
- panel_adjoint_total: bfloat16 [1024, 512, 512], P('row', 'col')
- input_adjoint: bfloat16 [1024, 512, 512], P('row', 'col')
The draws below stay inside these ranges and needn't reach their ends.
Inputs may be any that keep to these rules, and one draw needn't show every extreme that they name: `reader_row`: among the 32 rows of one device no reader index appears more than 2 times, and some index appears exactly 2 times. `diag_inverse`: lower triangular: zero above the diagonal, diagonal entries from 0.6 to 1.4.
All inputs are finite; a program needn't handle non-finite values.
Results may differ from the reference program's by a relative error of at most 0.0055.
Values may be sent and summed in bfloat16 or wider, within the bound.
A program may use at most 128 MiB of HBM per device.

```python
import math
import jax
import jax.numpy as jnp
import numpy as np
from jax import lax

WIDTH = 512
BLOCK_ROWS = 512
K_DEV = 32
S_DEV = 4
CAP = 2
KB = 1024
SB = 128
N_ROW = 32


def draw_diag_inverse(key, part):
    key_lower = jax.random.fold_in(key, 11)
    key_diag = jax.random.fold_in(key, 12)
    row_pos = lax.broadcasted_iota(jnp.int32, (WIDTH, WIDTH), 0)
    column_pos = lax.broadcasted_iota(jnp.int32, (WIDTH, WIDTH), 1)
    lower_part = jnp.clip(jax.random.normal(key_lower, (WIDTH, WIDTH), jnp.float32), -4.0, 4.0) * (0.8 / math.sqrt(WIDTH))
    diagonal = jax.random.uniform(key_diag, (WIDTH, WIDTH), jnp.float32, 0.6, 1.4)
    values = jnp.where(row_pos > column_pos, lower_part, jnp.where(row_pos == column_pos, diagonal, 0.0))
    return values.astype(jnp.bfloat16)


def plant(values, stream_key, least, high):
    spot = [jax.random.randint(jax.random.fold_in(stream_key, axis), (), 0, length) for axis, length in enumerate(values.shape)]
    widest = values.shape.index(max(values.shape))
    next_to = spot[:widest] + [(spot[widest] + 1) % values.shape[widest]] + spot[widest + 1:]
    return values.at[tuple(spot)].set(least).at[tuple(next_to)].set(high)


def block_levels(stream_key, shape, pieces, low, top_value):
    gain = 1.0
    for position, shards_of in pieces:
        steps = jax.random.uniform(jax.random.fold_in(jax.random.fold_in(stream_key, 6), position), (shards_of,), jnp.float32, low / len(pieces), top_value / len(pieces))
        gain = gain * jnp.repeat(jnp.exp(steps), shape[position] // shards_of).reshape((-1,) + (1,) * (len(shape) - 1 - position))
    return gain


def shared_out(rng, own, number, rows, amount, top, most, skew):
    sequence = jax.random.permutation(rng, amount)
    crowded, common = load_shares(amount, rows * top, most, skew, True), load_shares(amount, rows * top, most, skew, False)
    places = jnp.arange(amount)

    def named(sizes, turn):
        used = int((sizes > 0).sum())
        fixed = max(1, used // 4)
        moved = fixed + (places - fixed + turn * (used - fixed)) % max(1, amount - fixed)
        return jnp.zeros((amount,), jnp.int32).at[sequence[jnp.where(places < fixed, places, moved)]].set(jnp.asarray(sizes, jnp.int32))

    sizes = jnp.where(number % 4 == 0, named(crowded, number // 4), named(common, number - number // 4 - 1))
    mixed = jax.random.permutation(jax.random.fold_in(own, 3), amount)
    donor, taker = mixed[0:amount // 2 * 2:2], mixed[1:amount // 2 * 2:2]
    margin = jnp.minimum(sizes[donor] - 1, most - sizes[taker]) // 2
    margin = jnp.where((donor == sequence[0]) | (taker == sequence[0]) | (sizes[taker] == 0), 0, jnp.maximum(margin, 0))
    moved = jax.random.randint(jax.random.fold_in(own, 4), (amount // 2,), 0, 1 << 20) % (margin + 1)
    sizes = sizes.at[donor].add(-moved).at[taker].add(moved)
    items = jnp.searchsorted(jnp.cumsum(sizes), jnp.arange(rows * top), side="right").astype(jnp.int32)
    table = items.reshape(top, rows).T
    table = table[jax.random.permutation(jax.random.fold_in(own, 1), rows)]
    turn = jax.random.randint(jax.random.fold_in(own, 2), (rows, 1), 0, top)
    return jnp.take_along_axis(table, (jnp.arange(top)[None, :] + turn) % top, axis=1)


def load_shares(amount, total, most, slope, full):
    weights = [(1 << 20) // math.isqrt(standing ** slope) + 1 for standing in range(1, amount + 1)]
    largest = most if full else min(most, max(-(-total // amount), total * weights[0] // sum(weights)))
    least = 1 if total - largest >= amount - 1 else 0
    holding, rest = [largest] + [least] * (amount - 1), total - largest - least * (amount - 1)
    while rest > 0:
        candidates = [i for i in range(1, amount) if holding[i] < largest] or [i for i in range(1, amount) if holding[i] < most]
        pool, left = sum([weights[i] for i in candidates]), rest
        for i in candidates:
            more = min(most - holding[i], max(1, left * weights[i] // pool), rest)
            holding[i] = holding[i] + more
            rest = rest - more
    return np.array(holding)


def bell_draw(own_key, shape, spread, bound, split=(), held_as=jnp.bfloat16):
    entries = jax.random.normal(own_key, shape, jnp.float32) * spread
    if len(split) > 0:
        entries = block_levels(own_key, shape, split, -0.22, 0.18) * entries
    return jnp.clip(entries, min=-bound, max=bound).astype(held_as)


def setup_inputs(seed: int = 0) -> dict:
    seeds = jax.random.split(jax.random.key(seed), 7)
    panels = bell_draw(seeds[0], (KB, WIDTH, BLOCK_ROWS), 1.0, 6.0, ((0, 32), (1, 8)))
    reader_row_keys = jax.random.split(jax.random.fold_in(seeds[1], 1), KB // K_DEV)
    reader_row_turns = jax.random.permutation(jax.random.fold_in(seeds[1], 3), KB // K_DEV)
    reader_row = jax.vmap(lambda own, number: shared_out(jax.random.fold_in(seeds[1], 2), own, number, K_DEV, N_ROW, 1, CAP, 2))(reader_row_keys, reader_row_turns).reshape((KB, 1))
    tile_offset = plant(jax.random.randint(seeds[2], (KB,), 0, S_DEV), jax.random.fold_in(seeds[2], 1), 0, S_DEV - 1).astype(jnp.int32)
    schur_adjoint = bell_draw(seeds[3], (SB, BLOCK_ROWS, BLOCK_ROWS), (2 * BLOCK_ROWS) ** -0.5, 0.1875, ((0, 32),))
    panel_adjoint = bell_draw(seeds[4], (KB, WIDTH, BLOCK_ROWS), 1.0, 6.0, ((0, 32), (1, 8)))
    diag_inverse = draw_diag_inverse(jax.random.fold_in(seeds[6], 71), 0)
    return dict(panels=panels, reader_row=reader_row, tile_offset=tile_offset, schur_adjoint=schur_adjoint, panel_adjoint=panel_adjoint, diag_inverse=diag_inverse)


def reference(panels, reader_row, tile_offset, schur_adjoint, panel_adjoint, diag_inverse):
    tile_index = (reader_row[:, 0] * S_DEV + tile_offset).astype(jnp.int32)
    group_count = KB // 8
    panel_groups = panels.reshape(group_count, 8, WIDTH, BLOCK_ROWS)
    index_groups = tile_index.reshape(group_count, 8)

    def adjoint(pair_args):
        block_group, tile_group = pair_args
        picked = schur_adjoint[tile_group].astype(jnp.float32)
        left_side = block_group.astype(jnp.float32)
        both_sides = jnp.einsum("nkr,nrs->nks", left_side, picked, precision=lax.Precision.HIGHEST)
        both_sides = both_sides + jnp.einsum("nkr,nsr->nks", left_side, picked, precision=lax.Precision.HIGHEST)
        return (-both_sides).astype(jnp.bfloat16)

    adjoint_blocks = lax.map(adjoint, (panel_groups, index_groups)).reshape(KB, WIDTH, BLOCK_ROWS)
    panel_adjoint_total = (panel_adjoint.astype(jnp.float32) + adjoint_blocks.astype(jnp.float32)).astype(jnp.bfloat16)
    stacked = jnp.transpose(panel_adjoint_total, (1, 0, 2)).reshape(WIDTH, KB * BLOCK_ROWS)
    product = jnp.dot(diag_inverse.astype(jnp.float32).T, stacked.astype(jnp.float32), precision=lax.Precision.HIGHEST)
    input_adjoint = jnp.transpose(product.reshape(WIDTH, KB, BLOCK_ROWS), (1, 0, 2)).astype(jnp.bfloat16)
    return (panel_adjoint_total, input_adjoint)
```

```python
import functools

import jax
import jax.numpy as jnp
from jax import lax
from jax.experimental import pallas as pl
from jax.experimental.pallas import tpu as pltpu
from jax.sharding import PartitionSpec as P

MESH = pl.DeviceIdType.MESH
BF16 = jnp.bfloat16
F32 = jnp.float32
STRIDE = 11
CHUNKS = 4
FIRST, SECOND, BLOCK_OF, READER_OF, RANK_OF, PLACE_OF = range(6)


def index_kernel(n, reader_ref, offset_ref, table_ref, tile_ref, count_ref):
    def clear(i, carry):
        table_ref[FIRST * n + i] = 0
        table_ref[SECOND * n + i] = 0
        tile_ref[0, i] = 0
        tile_ref[0, n + i] = 0
        count_ref[i] = 0
        return carry

    lax.fori_loop(0, n, clear, 0)

    def place(block, carry):
        early, late = carry
        reader = reader_ref[block, 0]
        rank = count_ref[reader]
        count_ref[reader] = rank + 1
        table_ref[rank * n + reader] = block
        tile_ref[0, rank * n + reader] = offset_ref[block]
        is_early = ((rank == 0) & (early < n // 2)).astype(jnp.int32)
        position = is_early * early + (1 - is_early) * (n // 2 + late)
        table_ref[BLOCK_OF * n + position] = block
        table_ref[READER_OF * n + position] = reader
        table_ref[RANK_OF * n + position] = rank
        table_ref[PLACE_OF * n + block] = position
        return early + is_early, late + 1 - is_early

    lax.fori_loop(0, n, place, (jnp.int32(0), jnp.int32(0)))


def partner(dims, me, step, receive):
    nx, ny, _ = dims
    x, y, core = me // (2 * ny), (me // 2) % ny, me % 2
    shift = (step * STRIDE) % (nx * ny * 2)
    dx, dy, dc = shift // (2 * ny), (shift // 2) % ny, shift % 2
    sign = 1 - 2 * core
    if receive:
        sign = sign * (2 * dc - 1)
    to_x, to_y = (x + sign * dx + nx) % nx, (y + sign * dy + ny) % ny
    return (to_x * ny + to_y) * 2 + (core + dc) % 2


def level_kernel(
    dims, cols, chunks,
    table, tile_row, panels, tiles, adjoint, diag,
    total_ref, input_ref,
    sums, diag_t, tile_in, tile_ids,
    out_0, out_1, in_0, in_1, *rest,
):
    n = dims[0] * dims[1] * dims[2]
    half = n // 2
    own = half // cols
    depth, width = panels.shape[1:]
    part = width // chunks
    outs, ins = (out_0, out_1), (in_0, in_1)
    rest = list(rest)

    def take(amount):
        got, rest[:] = rest[:amount], rest[amount:]
        return got

    product = (take(chunks), take(chunks))
    returned = (take(chunks), take(chunks))
    total = take(chunks)
    gathered = (take(chunks), take(chunks))
    solved = (take(chunks), take(chunks))
    result = take(chunks)
    (f_send, f_recv, r_send, r_recv, t_send, t_recv, i_send, i_recv, m_send, m_recv, d_send, d_recv, local) = rest

    row, col = lax.axis_index("row"), lax.axis_index("col")

    def remote(src, dst, send, recv, to_row, to_col):
        return pltpu.make_async_remote_copy(
            src_ref=src, dst_ref=dst, send_sem=send, recv_sem=recv,
            device_id=(to_row, to_col), device_id_type=MESH,
        )

    def wait_for(view, sem):
        pltpu.make_async_copy(view, view, sem).wait()

    def send_to(step):
        return partner(dims, row, step, False)

    def got_from(step):
        return partner(dims, row, step, True)

    def other_col(step):
        return (col + step) % cols

    barrier = pltpu.get_barrier_semaphore()

    @pl.loop(1, n)
    def _(step):
        pl.semaphore_signal(barrier, inc=1, device_id=(send_to(step), col), device_id_type=MESH)

    @pl.loop(1, cols)
    def _(step):
        pl.semaphore_signal(barrier, inc=1, device_id=(row, other_col(step)), device_id_type=MESH)

    pl.semaphore_wait(barrier, n - 1 + cols - 1)

    tile_in[row] = tile_row[...]

    def stage(rank, step):
        to = send_to(step)
        outs[rank][to] = panels[table[rank * n + to]]

    def send_slot(rank, step):
        to = send_to(step)
        remote(outs[rank].at[to], ins[rank].at[row], f_send.at[rank], f_recv.at[rank, row], to, col).start()

    @pl.loop(1, n)
    def _(step):
        to = send_to(step)
        remote(tile_in.at[row], tile_in.at[row], m_send, m_recv, to, col).start()
        stage(0, step)
        send_slot(0, step)

    mine = pl.ds(pl.multiple_of(col * depth, depth), depth)
    diag_t[mine, :] = diag[...].astype(F32).T.astype(BF16)

    @pl.loop(1, cols)
    def _(step):
        remote(diag_t.at[mine, :], diag_t.at[mine, :], d_send, d_recv, row, other_col(step)).start()

    side = 128

    @pl.loop(0, tiles.shape[0])
    def _(i):
        for a in range(0, width, side):
            for b in range(0, width, side):
                straight = tiles[i, a : a + side, b : b + side].astype(F32)
                turned = tiles[i, b : b + side, a : a + side].astype(F32).T
                sums[i, a : a + side, b : b + side] = (straight + turned).astype(BF16)

    @pl.loop(1, n)
    def _(step):
        stage(1, step)

    for rank in range(2):
        outs[rank][row] = panels[table[rank * n + row]]

    wait_for(tile_in.at[pl.ds(0, n - 1)], m_recv)
    ids = pltpu.make_async_copy(tile_in, tile_ids, local)
    ids.start()
    ids.wait()

    def multiply(rank, block, source, into):
        tile = tile_ids[source, 0, rank * n + row]
        value = jnp.dot(block, sums[tile], preferred_element_type=F32)
        value = (-value).astype(BF16)
        for j in range(chunks):
            into[rank][j][source] = value[:, j * part : (j + 1) * part]

    def give_back(rank, j, step):
        to = got_from(step)
        remote(product[rank][j].at[to], returned[rank][j].at[row], r_send.at[rank, j], r_recv.at[rank, j], to, col).start()

    def reader(rank):
        multiply(rank, outs[rank][row], row, returned)

        @pl.loop(1, n)
        def _(step):
            source = got_from(step)
            wait_for(ins[rank].at[source], f_recv.at[rank, source])
            multiply(rank, ins[rank][source], source, product)
            give_back(rank, 0, step)

        for j in range(1, chunks):

            @pl.loop(1, n)
            def _(step):
                give_back(rank, j, step)

    def add_up(group, j):
        wait_for(returned[group][j].at[pl.ds(0, n - 1)], r_recv.at[group, j])

        @pl.loop(group * half, (group + 1) * half)
        def _(position):
            block, slot = table[BLOCK_OF * n + position], table[READER_OF * n + position]
            term = returned[0][j][slot].astype(F32)
            if group:
                second = table[RANK_OF * n + position] > 0
                term = jnp.where(second, returned[1][j][slot].astype(F32), term)
            base = adjoint[block, :, j * part : (j + 1) * part].astype(F32)
            total[j][position] = (base + term).astype(BF16)

        @pl.loop(1, cols)
        def _(step):
            to = other_col(step)
            remote(
                total[j].at[pl.ds(group * half + to * own, own)], gathered[group][j].at[:, mine, :],
                t_send.at[group, j], t_recv.at[group, j], row, to,
            ).start()

        gathered[group][j][:, mine, :] = total[j][pl.ds(group * half + col * own, own)]

    def solve(group, j):
        wait_for(gathered[group][j].at[:, pl.ds(0, depth * (cols - 1)), :], t_recv.at[group, j])
        for q in range(own):
            value = jnp.dot(diag_t[...], gathered[group][j][q], preferred_element_type=F32)
            solved[group][j][q] = value.astype(BF16)
        places = pl.ds(group * half + col * own, own)

        @pl.loop(1, cols)
        def _(step):
            to = other_col(step)
            theirs = pl.ds(pl.multiple_of(to * depth, depth), depth)
            remote(
                solved[group][j].at[:, theirs, :], result[j].at[places],
                i_send.at[group, j], i_recv.at[group, j], row, to,
            ).start()

        result[j][places] = solved[group][j][:, mine, :]

    reader(0)

    @pl.loop(1, n)
    def _(step):
        send_slot(1, step)

    wait_for(diag_t.at[pl.ds(0, depth * (cols - 1)), :], d_recv)
    for j in range(chunks):
        add_up(0, j)
        if j:
            solve(0, j - 1)
    solve(0, chunks - 1)
    reader(1)
    for j in range(chunks):
        add_up(1, j)
        if j:
            solve(1, j - 1)

    @pl.loop(0, n)
    def _(block):
        place = table[PLACE_OF * n + block]
        for j in range(chunks):
            total_ref[block, :, j * part : (j + 1) * part] = total[j][place]

    solve(1, chunks - 1)

    for j in range(chunks):
        for group in range(2):
            wait_for(result[j].at[pl.ds(0, own * (cols - 1))], i_recv.at[group, j])

        @pl.loop(0, n)
        def _(block):
            input_ref[block, :, j * part : (j + 1) * part] = result[j][table[PLACE_OF * n + block]]

    wait_for(tile_in.at[pl.ds(0, n - 1)], m_send)
    wait_for(diag_t.at[pl.ds(0, depth * (cols - 1)), :], d_send)
    for rank in range(2):
        wait_for(outs[rank].at[pl.ds(0, n - 1)], f_send.at[rank])
        for j in range(chunks):
            wait_for(product[rank][j].at[pl.ds(0, n - 1)], r_send.at[rank, j])
            wait_for(result[j].at[pl.ds(0, own * (cols - 1))], t_send.at[rank, j])
            wait_for(result[j].at[pl.ds(0, own * (cols - 1))], i_send.at[rank, j])


def shards(dims, panels, reader_row, tile_offset, schur_adjoint, panel_adjoint, diag_inverse):
    cols = lax.axis_size("col")
    blocks, depth, width = panels.shape
    n, chunks = blocks, CHUNKS
    own, part = n // 2 // cols, width // chunks
    vmem, smem = pl.BlockSpec(memory_space=pltpu.VMEM), pl.BlockSpec(memory_space=pltpu.SMEM)
    table, tile_row = pl.pallas_call(
        functools.partial(index_kernel, n),
        out_shape=(
            jax.ShapeDtypeStruct((6 * n,), jnp.int32),
            jax.ShapeDtypeStruct((1, 128), jnp.int32),
        ),
        in_specs=[smem, smem],
        out_specs=(smem, smem),
        scratch_shapes=[pltpu.SMEM((n,), jnp.int32)],
    )(reader_row, tile_offset)
    slots = pltpu.VMEM((n, depth, width), BF16)
    slot_part = pltpu.VMEM((n, depth, part), BF16)
    owned = pltpu.VMEM((own, depth * cols, part), BF16)
    dma = pltpu.SemaphoreType.DMA
    return pl.pallas_call(
        functools.partial(level_kernel, dims, cols, chunks),
        out_shape=(
            jax.ShapeDtypeStruct(panels.shape, BF16),
            jax.ShapeDtypeStruct(panels.shape, BF16),
        ),
        in_specs=[smem, vmem, vmem, vmem, vmem, vmem],
        out_specs=(vmem, vmem),
        scratch_shapes=[
            pltpu.VMEM(schur_adjoint.shape, BF16),
            pltpu.VMEM((depth * cols, depth * cols), BF16),
            pltpu.VMEM((n, 1, 128), jnp.int32),
            pltpu.SMEM((n, 1, 128), jnp.int32),
            *[slots] * 4,
            *[slot_part] * (4 * chunks),
            *[slot_part] * chunks,
            *[owned] * (4 * chunks),
            *[slot_part] * chunks,
            dma((2,)),
            dma((2, n)),
            *[dma((2, chunks))] * 6,
            *[dma] * 5,
        ],
        compiler_params=pltpu.CompilerParams(
            collective_id=0, has_side_effects=True, vmem_limit_bytes=58 * 2**20
        ),
        cost_estimate=pl.CostEstimate(
            flops=4 * n * depth * width * width, bytes_accessed=10 * 2**20, transcendentals=0
        ),
    )(table, tile_row, panels, schur_adjoint, panel_adjoint, diag_inverse)


def solution(mesh):
    side = int(round((mesh.shape["row"] // 2) ** 0.5))
    in_specs = (
        P("row", "col", None),
        P("row", None),
        P("row"),
        P("row", None, None),
        P("row", "col", None),
        P(None, "col"),
    )
    out_specs = (P("row", "col", None), P("row", "col", None))
    return jax.shard_map(
        functools.partial(shards, (side, side, 2)),
        mesh=mesh, in_specs=in_specs, out_specs=out_specs, check_vma=False,
    )
```

```python
import functools

import jax
import jax.numpy as jnp
from jax import lax
from jax.experimental import pallas as pl
from jax.experimental.pallas import tpu as pltpu
from jax.sharding import PartitionSpec as P

MESH = pl.DeviceIdType.MESH
HBM = pltpu.MemorySpace.HBM
BF16 = jnp.bfloat16
F32 = jnp.float32
STRIDE = 11
AHEAD = 2
CHUNKS = 4
FIRST, SECOND, BLOCK_OF, READER_OF, RANK_OF, PLACE_OF, TILES = range(7)


def fill_tables(n, reader_ref, offset_ref, table_ref):
    sub = lax.broadcasted_iota(jnp.int32, (n, n), 0)
    lane = lax.broadcasted_iota(jnp.int32, (n, n), 1)

    def count(mask, axis):
        return jnp.sum(mask.astype(jnp.int32), axis=axis, keepdims=True)

    def pick(mask, values):
        return jnp.sum(jnp.where(mask, values, 0), axis=0, keepdims=True)

    def upright(values):
        return jnp.sum(jnp.where(sub == lane, values, 0), axis=1, keepdims=True)

    reader_row = jnp.broadcast_to(reader_ref[...], (n, n))
    reader = jnp.broadcast_to(upright(reader_row), (n, n))
    offset = jnp.broadcast_to(upright(jnp.broadcast_to(offset_ref[...], (n, n))), (n, n))
    same = reader == reader_row
    rank = jnp.broadcast_to(count(same & (lane < sub), 1), (n, n))
    rank_row = jnp.broadcast_to(count(same & (sub < lane), 0), (n, n))
    firsts = jnp.broadcast_to(count((rank_row == 0) & (lane < sub), 1), (n, n))
    firsts_row = jnp.broadcast_to(count((rank == 0) & (sub < lane), 0), (n, n))
    early = (rank == 0) & (firsts < n // 2)
    early_row = (rank_row == 0) & (firsts_row < n // 2)
    late = jnp.broadcast_to(count(jnp.logical_not(early_row) & (lane < sub), 1), (n, n))
    late_row = jnp.broadcast_to(count(jnp.logical_not(early) & (sub < lane), 0), (n, n))
    place = jnp.where(early, firsts, n // 2 + late)
    place_row = jnp.where(early_row, firsts_row, n // 2 + late_row)
    here = place == lane
    for rank_is, row in ((0, FIRST), (1, SECOND)):
        named = (reader == lane) & (rank == rank_is)
        table_ref[row, :, 0:n] = pick(named, sub)
        table_ref[TILES, :, rank_is * n : (rank_is + 1) * n] = pick(named, offset)
    table_ref[BLOCK_OF, :, 0:n] = pick(here, sub)
    table_ref[READER_OF, :, 0:n] = pick(here, reader)
    table_ref[RANK_OF, :, 0:n] = pick(here, rank)
    table_ref[PLACE_OF, :, 0:n] = jnp.minimum(place_row[0:1, :], n - 1)


def partner(dims, me, step, receive):
    nx, ny, _ = dims
    x, y, core = me // (2 * ny), (me // 2) % ny, me % 2
    shift = (step * STRIDE) % (nx * ny * 2)
    dx, dy, dc = shift // (2 * ny), (shift // 2) % ny, shift % 2
    sign = 1 - 2 * core
    if receive:
        sign = sign * (2 * dc - 1)
    to_x, to_y = (x + sign * dx + nx) % nx, (y + sign * dy + ny) % ny
    return (to_x * ny + to_y) * 2 + (core + dc) % 2


def level_kernel(
    dims, cols, chunks,
    reader_ref, offset_ref, panels_in, tiles_hbm, adjoint_in, diag_in,
    total_ref, input_ref,
    table_v, table, panels, tiles, adjoint, sums, diag_t, tile_in, tile_ids,
    out_0, out_1, in_0, in_1, *rest,
):
    n = dims[0] * dims[1] * dims[2]
    half = n // 2
    own = half // cols
    depth, width = panels.shape[1:]
    part = width // chunks
    outs, ins = (out_0, out_1), (in_0, in_1)
    rest = list(rest)

    def take(amount):
        got, rest[:] = rest[:amount], rest[amount:]
        return got

    product = (take(chunks), take(chunks))
    returned = (take(chunks), take(chunks))
    total = take(chunks)
    gathered = (take(chunks), take(chunks))
    solved = (take(chunks), take(chunks))
    result = take(chunks)
    (f_send, f_recv, r_send, r_recv, t_send, t_recv, i_send, i_recv, m_send, m_recv, d_send, d_recv, local, load) = rest

    row, col = lax.axis_index("row"), lax.axis_index("col")

    def remote(src, dst, send, recv, to_row, to_col):
        return pltpu.make_async_remote_copy(
            src_ref=src, dst_ref=dst, send_sem=send, recv_sem=recv,
            device_id=(to_row, to_col), device_id_type=MESH,
        )

    def wait_for(view, sem):
        pltpu.make_async_copy(view, view, sem).wait()

    def send_to(step):
        return partner(dims, row, step, False)

    def got_from(step):
        return partner(dims, row, step, True)

    def other_col(step):
        return (col + cols // 2 + (step // 2) * (2 * (step % 2) - 1) + cols) % cols

    mine = pl.ds(pl.multiple_of(col * depth, depth), depth)
    loads = [
        pltpu.make_async_copy(src, dst, load.at[i])
        for i, (src, dst) in enumerate(
            (
                (panels_in, panels),
                (tiles_hbm, tiles),
                (diag_in, diag_t.at[mine, :]),
                (adjoint_in, adjoint),
            )
        )
    ]
    for copy in loads:
        copy.start()

    barrier = pltpu.get_barrier_semaphore()

    @pl.loop(1, n)
    def _(step):
        pl.semaphore_signal(barrier, inc=1, device_id=(send_to(step), col), device_id_type=MESH)

    @pl.loop(1, cols)
    def _(step):
        pl.semaphore_signal(barrier, inc=1, device_id=(row, other_col(step)), device_id_type=MESH)

    fill_tables(n, reader_ref, offset_ref, table_v)
    tables = pltpu.make_async_copy(table_v, table, local)
    tables.start()
    tile_in[row] = table_v[TILES]
    tables.wait()
    loads[0].wait()

    def stage(rank):
        @pl.loop(0, n)
        def _(to):
            outs[rank][to] = panels[table[rank, 0, to]]

    stage(0)
    pl.semaphore_wait(barrier, n - 1 + cols - 1)

    def send_slot(rank, step):
        to = send_to(step)
        remote(outs[rank].at[to], ins[rank].at[row], f_send.at[rank], f_recv.at[rank, row], to, col).start()

    def send_slots(rank):
        @pl.loop(1, n)
        def _(step):
            send_slot(rank, step)

    @pl.loop(1, n)
    def _(step):
        remote(tile_in.at[row], tile_in.at[row], m_send, m_recv, send_to(step), col).start()

    send_slots(0)

    loads[2].wait()

    @pl.loop(1, cols)
    def _(step):
        remote(diag_t.at[mine, :], diag_t.at[mine, :], d_send, d_recv, row, other_col(step)).start()

    loads[1].wait()
    side = 128

    @pl.loop(0, tiles.shape[0])
    def _(i):
        for a in range(0, width, side):
            for b in range(0, width, side):
                straight = tiles[i, a : a + side, b : b + side].astype(F32)
                turned = tiles[i, b : b + side, a : a + side].astype(F32).T
                sums[i, a : a + side, b : b + side] = (straight + turned).astype(BF16)

    stage(1)
    wait_for(tile_in.at[pl.ds(0, n - 1)], m_recv)
    ids = pltpu.make_async_copy(tile_in, tile_ids, local)
    ids.start()
    ids.wait()

    def multiply(rank, block, source, into):
        tile = tile_ids[source, 0, rank * n + row]
        term = jnp.dot(block, sums[tile], preferred_element_type=F32)
        term = (-term).astype(BF16)
        for j in range(chunks):
            into[rank][j][source] = term[:, j * part : (j + 1) * part]

    halves = ((1, half), (half, n))

    def give_back(rank, j, step, h):
        to = got_from(step)
        remote(product[rank][j].at[to], returned[rank][j].at[row], r_send.at[rank, j, h], r_recv.at[rank, j], to, col).start()

    def gone(rank, j, h):
        first, last = halves[h]
        wait_for(product[rank][j].at[pl.ds(0, last - first)], r_send.at[rank, j, h])

    def reader(rank, h):
        @pl.loop(*halves[h])
        def _(step):
            source = got_from(step)
            wait_for(ins[rank].at[source], f_recv.at[rank, source])
            multiply(rank, ins[rank][source], source, product)
            give_back(rank, 0, step, h)

    def follow(rank, j):
        for h in range(2):
            gone(rank, j - 1, h)

            @pl.loop(*halves[h])
            def _(step):
                give_back(rank, j, step, h)

    def add_up(group, j):
        wait_for(returned[group][j].at[pl.ds(0, n - 1)], r_recv.at[group, j])

        @pl.loop(group * half, (group + 1) * half)
        def _(position):
            block, slot = table[BLOCK_OF, 0, position], table[READER_OF, 0, position]
            term = returned[0][j][slot].astype(F32)
            if group:
                second = table[RANK_OF, 0, position] > 0
                term = jnp.where(second, returned[1][j][slot].astype(F32), term)
            base = adjoint[block, :, j * part : (j + 1) * part].astype(F32)
            total[j][position] = (base + term).astype(BF16)

        @pl.loop(1, cols)
        def _(step):
            to = other_col(step)
            remote(
                total[j].at[pl.ds(group * half + to * own, own)], gathered[group][j].at[:, mine, :],
                t_send.at[group, j], t_recv.at[group, j], row, to,
            ).start()

        gathered[group][j][:, mine, :] = total[j][pl.ds(group * half + col * own, own)]

    def solve(group, j):
        wait_for(gathered[group][j].at[:, pl.ds(0, depth * (cols - 1)), :], t_recv.at[group, j])
        for q in range(own):
            value = jnp.dot(diag_t[...], gathered[group][j][q], preferred_element_type=F32)
            solved[group][j][q] = value.astype(BF16)
        places = pl.ds(group * half + col * own, own)

        @pl.loop(1, cols)
        def _(step):
            to = other_col(step)
            theirs = pl.ds(pl.multiple_of(to * depth, depth), depth)
            remote(
                solved[group][j].at[:, theirs, :], result[j].at[places],
                i_send.at[group, j], i_recv.at[group, j], row, to,
            ).start()

        result[j][places] = solved[group][j][:, mine, :]

    reader(0, 0)
    reader(0, 1)
    multiply(0, outs[0][row], row, returned)
    wait_for(diag_t.at[pl.ds(0, depth * (cols - 1)), :], d_recv)
    loads[3].wait()
    for j in range(chunks):
        if j + 1 < chunks:
            follow(0, j + 1)
        else:
            send_slots(1)
        add_up(0, j)
        if j >= AHEAD:
            solve(0, j - AHEAD)
    for j in range(chunks - AHEAD, chunks - 1):
        solve(0, j)
    reader(1, 0)
    solve(0, chunks - 1)
    reader(1, 1)
    multiply(1, outs[1][row], row, returned)
    for j in range(chunks):
        if j + 1 < chunks:
            follow(1, j + 1)
        add_up(1, j)
        if j >= AHEAD:
            solve(1, j - AHEAD)

    @pl.loop(0, n)
    def _(block):
        place = table[PLACE_OF, 0, block]
        for j in range(chunks):
            total_ref[block, :, j * part : (j + 1) * part] = total[j][place]

    for j in range(chunks - AHEAD, chunks):
        solve(1, j)

    for j in range(chunks):
        for group in range(2):
            wait_for(result[j].at[pl.ds(0, own * (cols - 1))], i_recv.at[group, j])

        @pl.loop(0, n)
        def _(block):
            input_ref[block, :, j * part : (j + 1) * part] = result[j][table[PLACE_OF, 0, block]]

    wait_for(tile_in.at[pl.ds(0, n - 1)], m_send)
    wait_for(diag_t.at[pl.ds(0, depth * (cols - 1)), :], d_send)
    for rank in range(2):
        wait_for(outs[rank].at[pl.ds(0, n - 1)], f_send.at[rank])
        for h in range(2):
            gone(rank, chunks - 1, h)
        for j in range(chunks):
            wait_for(result[j].at[pl.ds(0, own * (cols - 1))], t_send.at[rank, j])
            wait_for(result[j].at[pl.ds(0, own * (cols - 1))], i_send.at[rank, j])


def shards(dims, panels, reader_row, tile_offset, schur_adjoint, panel_adjoint, diag_inverse):
    cols = lax.axis_size("col")
    blocks, depth, width = panels.shape
    n, chunks = blocks, CHUNKS
    own, part = n // 2 // cols, width // chunks
    vmem, hbm = pl.BlockSpec(memory_space=pltpu.VMEM), pl.BlockSpec(memory_space=HBM)
    slots = pltpu.VMEM((n, depth, width), BF16)
    slot_part = pltpu.VMEM((n, depth, part), BF16)
    owned = pltpu.VMEM((own, depth * cols, part), BF16)
    dma = pltpu.SemaphoreType.DMA
    return pl.pallas_call(
        functools.partial(level_kernel, dims, cols, chunks),
        out_shape=(
            jax.ShapeDtypeStruct(panels.shape, BF16),
            jax.ShapeDtypeStruct(panels.shape, BF16),
        ),
        in_specs=[vmem, vmem, hbm, hbm, hbm, hbm],
        out_specs=(vmem, vmem),
        scratch_shapes=[
            pltpu.VMEM((TILES + 1, 1, 128), jnp.int32),
            pltpu.SMEM((TILES + 1, 1, 128), jnp.int32),
            pltpu.VMEM(panels.shape, BF16),
            pltpu.VMEM(schur_adjoint.shape, BF16),
            pltpu.VMEM(panels.shape, BF16),
            pltpu.VMEM(schur_adjoint.shape, BF16),
            pltpu.VMEM((depth * cols, depth * cols), BF16),
            pltpu.VMEM((n, 1, 128), jnp.int32),
            pltpu.SMEM((n, 1, 128), jnp.int32),
            *[slots] * 4,
            *[slot_part] * (4 * chunks),
            *[slot_part] * chunks,
            *[owned] * (4 * chunks),
            *[slot_part] * chunks,
            dma((2,)),
            dma((2, n)),
            dma((2, chunks, 2)),
            *[dma((2, chunks))] * 5,
            *[dma] * 5,
            dma((4,)),
        ],
        compiler_params=pltpu.CompilerParams(
            collective_id=0, has_side_effects=True, vmem_limit_bytes=58 * 2**20
        ),
        cost_estimate=pl.CostEstimate(
            flops=4 * n * depth * width * width, bytes_accessed=10 * 2**20, transcendentals=0
        ),
    )(
        reader_row.reshape(1, n), tile_offset.reshape(1, n),
        panels, schur_adjoint, panel_adjoint, diag_inverse.T,
    )


def solution(mesh):
    side = int(round((mesh.shape["row"] // 2) ** 0.5))
    in_specs = (
        P("row", "col", None),
        P("row", None),
        P("row"),
        P("row", None, None),
        P("row", "col", None),
        P(None, "col"),
    )
    out_specs = (P("row", "col", None), P("row", "col", None))
    return jax.shard_map(
        functools.partial(shards, (side, side, 2)),
        mesh=mesh, in_specs=in_specs, out_specs=out_specs, check_vma=False,
    )
```

```python
import functools

import jax
import jax.numpy as jnp
from jax import lax
from jax.experimental import pallas as pl
from jax.experimental.pallas import tpu as pltpu
from jax.sharding import PartitionSpec as P

MESH = pl.DeviceIdType.MESH
HBM = pltpu.MemorySpace.HBM
BF16 = jnp.bfloat16
F32 = jnp.float32
STRIDE = 11
AHEAD = 2
CHUNKS = 4
FIRST, SECOND, BLOCK_OF, READER_OF, RANK_OF, PLACE_OF, TILES = range(7)


def fill_tables(n, reader_ref, offset_ref, table_ref):
    sub = lax.broadcasted_iota(jnp.int32, (n, n), 0)
    lane = lax.broadcasted_iota(jnp.int32, (n, n), 1)

    def count(mask, axis):
        return jnp.sum(mask.astype(jnp.int32), axis=axis, keepdims=True)

    def pick(mask, values):
        return jnp.sum(jnp.where(mask, values, 0), axis=0, keepdims=True)

    def upright(values):
        return jnp.sum(jnp.where(sub == lane, values, 0), axis=1, keepdims=True)

    reader_row = jnp.broadcast_to(reader_ref[...], (n, n))
    reader = jnp.broadcast_to(upright(reader_row), (n, n))
    offset = jnp.broadcast_to(upright(jnp.broadcast_to(offset_ref[...], (n, n))), (n, n))
    same = reader == reader_row
    rank = jnp.broadcast_to(count(same & (lane < sub), 1), (n, n))
    rank_row = jnp.broadcast_to(count(same & (sub < lane), 0), (n, n))
    firsts = jnp.broadcast_to(count((rank_row == 0) & (lane < sub), 1), (n, n))
    firsts_row = jnp.broadcast_to(count((rank == 0) & (sub < lane), 0), (n, n))
    early = (rank == 0) & (firsts < n // 2)
    early_row = (rank_row == 0) & (firsts_row < n // 2)
    late = jnp.broadcast_to(count(jnp.logical_not(early_row) & (lane < sub), 1), (n, n))
    late_row = jnp.broadcast_to(count(jnp.logical_not(early) & (sub < lane), 0), (n, n))
    place = jnp.where(early, firsts, n // 2 + late)
    place_row = jnp.where(early_row, firsts_row, n // 2 + late_row)
    here = place == lane
    for rank_is, row in ((0, FIRST), (1, SECOND)):
        named = (reader == lane) & (rank == rank_is)
        table_ref[row, :, 0:n] = pick(named, sub)
        table_ref[TILES, :, rank_is * n : (rank_is + 1) * n] = pick(named, offset)
    table_ref[BLOCK_OF, :, 0:n] = pick(here, sub)
    table_ref[READER_OF, :, 0:n] = pick(here, reader)
    table_ref[RANK_OF, :, 0:n] = pick(here, rank)
    table_ref[PLACE_OF, :, 0:n] = jnp.minimum(place_row[0:1, :], n - 1)


def partner(dims, me, step, receive):
    nx, ny, _ = dims
    x, y, core = me // (2 * ny), (me // 2) % ny, me % 2
    shift = (step * STRIDE) % (nx * ny * 2)
    dx, dy, dc = shift // (2 * ny), (shift // 2) % ny, shift % 2
    sign = 1 - 2 * core
    if receive:
        sign = sign * (2 * dc - 1)
    to_x, to_y = (x + sign * dx + nx) % nx, (y + sign * dy + ny) % ny
    return (to_x * ny + to_y) * 2 + (core + dc) % 2


def level_kernel(
    dims, cols, chunks,
    reader_ref, offset_ref, panels_in, tiles_hbm, adjoint_in, diag_in,
    total_ref, input_ref,
    table_v, table, panels, tiles, adjoint, sums, diag_t, tile_in, tile_ids,
    out_0, out_1, in_0, in_1, *rest,
):
    n = dims[0] * dims[1] * dims[2]
    half = n // 2
    own = half // cols
    depth, width = panels.shape[1:]
    part = width // chunks
    outs, ins = (out_0, out_1), (in_0, in_1)
    rest = list(rest)

    def take(amount):
        got, rest[:] = rest[:amount], rest[amount:]
        return got

    product = (take(chunks), take(chunks))
    returned = (take(chunks), take(chunks))
    total = take(chunks)
    gathered = (take(chunks), take(chunks))
    solved = (take(chunks), take(chunks))
    result = take(chunks)
    (f_send, f_recv, r_send, r_recv, t_send, t_recv, i_send, i_recv, m_send, m_recv, d_send, d_recv, local, load) = rest

    row, col = lax.axis_index("row"), lax.axis_index("col")

    def remote(src, dst, send, recv, to_row, to_col):
        return pltpu.make_async_remote_copy(
            src_ref=src, dst_ref=dst, send_sem=send, recv_sem=recv,
            device_id=(to_row, to_col), device_id_type=MESH,
        )

    def wait_for(view, sem):
        pltpu.make_async_copy(view, view, sem).wait()

    def send_to(step):
        return partner(dims, row, step, False)

    def got_from(step):
        return partner(dims, row, step, True)

    def other_col(step):
        return (col + cols // 2 + (step // 2) * (2 * (step % 2) - 1) + cols) % cols

    mine = pl.ds(pl.multiple_of(col * depth, depth), depth)
    loads = [
        pltpu.make_async_copy(src, dst, load.at[i])
        for i, (src, dst) in enumerate(
            (
                (panels_in, panels),
                (tiles_hbm, tiles),
                (diag_in, diag_t.at[mine, :]),
                (adjoint_in, adjoint),
            )
        )
    ]
    for copy in loads:
        copy.start()

    barrier = pltpu.get_barrier_semaphore()

    @pl.loop(1, n)
    def _(step):
        pl.semaphore_signal(barrier, inc=1, device_id=(send_to(step), col), device_id_type=MESH)

    @pl.loop(1, cols)
    def _(step):
        pl.semaphore_signal(barrier, inc=1, device_id=(row, other_col(step)), device_id_type=MESH)

    fill_tables(n, reader_ref, offset_ref, table_v)
    tables = pltpu.make_async_copy(table_v, table, local)
    tables.start()
    tile_in[row] = table_v[TILES]
    tables.wait()
    loads[0].wait()

    def stage(rank):
        @pl.loop(0, n)
        def _(to):
            outs[rank][to] = panels[table[rank, 0, to]]

    stage(0)
    pl.semaphore_wait(barrier, n - 1 + cols - 1)

    def send_slot(rank, step):
        to = send_to(step)
        remote(outs[rank].at[to], ins[rank].at[row], f_send.at[rank], f_recv.at[rank, row], to, col).start()

    def send_slots(rank):
        @pl.loop(1, n)
        def _(step):
            send_slot(rank, step)

    @pl.loop(1, n)
    def _(step):
        remote(tile_in.at[row], tile_in.at[row], m_send, m_recv, send_to(step), col).start()
        send_slot(0, step)

    loads[2].wait()

    @pl.loop(1, cols)
    def _(step):
        remote(diag_t.at[mine, :], diag_t.at[mine, :], d_send, d_recv, row, other_col(step)).start()

    loads[1].wait()
    side = 128

    @pl.loop(0, tiles.shape[0])
    def _(i):
        for a in range(0, width, side):
            for b in range(0, width, side):
                straight = tiles[i, a : a + side, b : b + side].astype(F32)
                turned = tiles[i, b : b + side, a : a + side].astype(F32).T
                sums[i, a : a + side, b : b + side] = (straight + turned).astype(BF16)

    stage(1)
    wait_for(tile_in.at[pl.ds(0, n - 1)], m_recv)
    ids = pltpu.make_async_copy(tile_in, tile_ids, local)
    ids.start()
    ids.wait()

    def multiply(rank, block, source, into):
        tile = tile_ids[source, 0, rank * n + row]
        term = jnp.dot(block, sums[tile], preferred_element_type=F32)
        term = (-term).astype(BF16)
        for j in range(chunks):
            into[rank][j][source] = term[:, j * part : (j + 1) * part]

    halves = ((1, half), (half, n))

    def give_back(rank, j, step, h):
        to = got_from(step)
        remote(product[rank][j].at[to], returned[rank][j].at[row], r_send.at[rank, j, h], r_recv.at[rank, j], to, col).start()

    def gone(rank, j, h):
        first, last = halves[h]
        wait_for(product[rank][j].at[pl.ds(0, last - first)], r_send.at[rank, j, h])

    def reader(rank, h):
        @pl.loop(*halves[h])
        def _(step):
            source = got_from(step)
            wait_for(ins[rank].at[source], f_recv.at[rank, source])
            multiply(rank, ins[rank][source], source, product)
            give_back(rank, 0, step, h)

    def follow(rank, j):
        for h in range(2):
            gone(rank, j - 1, h)

            @pl.loop(*halves[h])
            def _(step):
                give_back(rank, j, step, h)

    def add_up(group, j):
        wait_for(returned[group][j].at[pl.ds(0, n - 1)], r_recv.at[group, j])

        @pl.loop(group * half, (group + 1) * half)
        def _(position):
            block, slot = table[BLOCK_OF, 0, position], table[READER_OF, 0, position]
            term = returned[0][j][slot].astype(F32)
            if group:
                second = table[RANK_OF, 0, position] > 0
                term = jnp.where(second, returned[1][j][slot].astype(F32), term)
            base = adjoint[block, :, j * part : (j + 1) * part].astype(F32)
            total[j][position] = (base + term).astype(BF16)

        @pl.loop(1, cols)
        def _(step):
            to = other_col(step)
            remote(
                total[j].at[pl.ds(group * half + to * own, own)], gathered[group][j].at[:, mine, :],
                t_send.at[group, j], t_recv.at[group, j], row, to,
            ).start()

        gathered[group][j][:, mine, :] = total[j][pl.ds(group * half + col * own, own)]

    def solve(group, j):
        wait_for(gathered[group][j].at[:, pl.ds(0, depth * (cols - 1)), :], t_recv.at[group, j])
        for q in range(own):
            value = jnp.dot(diag_t[...], gathered[group][j][q], preferred_element_type=F32)
            solved[group][j][q] = value.astype(BF16)
        places = pl.ds(group * half + col * own, own)

        @pl.loop(1, cols)
        def _(step):
            to = other_col(step)
            theirs = pl.ds(pl.multiple_of(to * depth, depth), depth)
            remote(
                solved[group][j].at[:, theirs, :], result[j].at[places],
                i_send.at[group, j], i_recv.at[group, j], row, to,
            ).start()

        result[j][places] = solved[group][j][:, mine, :]

    reader(0, 0)
    reader(0, 1)
    multiply(0, outs[0][row], row, returned)
    wait_for(diag_t.at[pl.ds(0, depth * (cols - 1)), :], d_recv)
    loads[3].wait()
    for j in range(chunks):
        if j + 1 < chunks:
            follow(0, j + 1)
        else:
            send_slots(1)
        add_up(0, j)
        if j >= AHEAD:
            solve(0, j - AHEAD)
    for j in range(chunks - AHEAD, chunks - 1):
        solve(0, j)
    reader(1, 0)
    solve(0, chunks - 1)
    reader(1, 1)
    multiply(1, outs[1][row], row, returned)
    for j in range(chunks):
        if j + 1 < chunks:
            follow(1, j + 1)
        add_up(1, j)
        if j >= AHEAD:
            solve(1, j - AHEAD)

    @pl.loop(0, n)
    def _(block):
        place = table[PLACE_OF, 0, block]
        for j in range(chunks):
            total_ref[block, :, j * part : (j + 1) * part] = total[j][place]

    for j in range(chunks - AHEAD, chunks):
        solve(1, j)

    for j in range(chunks):
        for group in range(2):
            wait_for(result[j].at[pl.ds(0, own * (cols - 1))], i_recv.at[group, j])

        @pl.loop(0, n)
        def _(block):
            input_ref[block, :, j * part : (j + 1) * part] = result[j][table[PLACE_OF, 0, block]]

    wait_for(tile_in.at[pl.ds(0, n - 1)], m_send)
    wait_for(diag_t.at[pl.ds(0, depth * (cols - 1)), :], d_send)
    for rank in range(2):
        wait_for(outs[rank].at[pl.ds(0, n - 1)], f_send.at[rank])
        for h in range(2):
            gone(rank, chunks - 1, h)
        for j in range(chunks):
            wait_for(result[j].at[pl.ds(0, own * (cols - 1))], t_send.at[rank, j])
            wait_for(result[j].at[pl.ds(0, own * (cols - 1))], i_send.at[rank, j])


def shards(dims, panels, reader_row, tile_offset, schur_adjoint, panel_adjoint, diag_inverse):
    cols = lax.axis_size("col")
    blocks, depth, width = panels.shape
    n, chunks = blocks, CHUNKS
    own, part = n // 2 // cols, width // chunks
    vmem, hbm = pl.BlockSpec(memory_space=pltpu.VMEM), pl.BlockSpec(memory_space=HBM)
    slots = pltpu.VMEM((n, depth, width), BF16)
    slot_part = pltpu.VMEM((n, depth, part), BF16)
    owned = pltpu.VMEM((own, depth * cols, part), BF16)
    dma = pltpu.SemaphoreType.DMA
    return pl.pallas_call(
        functools.partial(level_kernel, dims, cols, chunks),
        out_shape=(pltpu.VMEM(panels.shape, BF16), pltpu.VMEM(panels.shape, BF16)),
        in_specs=[vmem, vmem, hbm, hbm, hbm, hbm],
        out_specs=(vmem, vmem),
        scratch_shapes=[
            pltpu.VMEM((TILES + 1, 1, 128), jnp.int32),
            pltpu.SMEM((TILES + 1, 1, 128), jnp.int32),
            pltpu.VMEM(panels.shape, BF16),
            pltpu.VMEM(schur_adjoint.shape, BF16),
            pltpu.VMEM(panels.shape, BF16),
            pltpu.VMEM(schur_adjoint.shape, BF16),
            pltpu.VMEM((depth * cols, depth * cols), BF16),
            pltpu.VMEM((n, 1, 128), jnp.int32),
            pltpu.SMEM((n, 1, 128), jnp.int32),
            *[slots] * 4,
            *[slot_part] * (4 * chunks),
            *[slot_part] * chunks,
            *[owned] * (4 * chunks),
            *[slot_part] * chunks,
            dma((2,)),
            dma((2, n)),
            dma((2, chunks, 2)),
            *[dma((2, chunks))] * 5,
            *[dma] * 5,
            dma((4,)),
        ],
        compiler_params=pltpu.CompilerParams(
            collective_id=0, has_side_effects=True, vmem_limit_bytes=54 * 2**20
        ),
        cost_estimate=pl.CostEstimate(
            flops=4 * n * depth * width * width, bytes_accessed=10 * 2**20, transcendentals=0
        ),
    )(
        reader_row.reshape(1, n), tile_offset.reshape(1, n),
        panels, schur_adjoint, panel_adjoint, diag_inverse.T,
    )


def solution(mesh):
    side = int(round((mesh.shape["row"] // 2) ** 0.5))
    in_specs = (
        P("row", "col", None),
        P("row", None),
        P("row"),
        P("row", None, None),
        P("row", "col", None),
        P(None, "col"),
    )
    out_specs = (P("row", "col", None), P("row", "col", None))
    return jax.shard_map(
        functools.partial(shards, (side, side, 2)),
        mesh=mesh, in_specs=in_specs, out_specs=out_specs, check_vma=False,
    )
```
